32 devices in a mesh: frame: 8 (over z, x), freq: 4 (over y, core).
Axes of the slice: x: 2, y: 2, z: 4, core: 2. Of those that a mesh axis runs over, the one named last changes fastest.
Arguments:
- spectrum: float32 [8192, 4096], P('freq', 'frame'), may hold values from 0.1 to 10
- basis: float32 [8192, 128], P(('freq', 'frame')), may hold values from 0.02 to 0.5
- activations: float32 [4096, 128], P(('frame', 'freq')), may hold values from 0.02 to 0.5
Outputs:
- basis_out: float32 [8192, 128], P(('freq', 'frame'))
- activations_out: float32 [4096, 128], P(('frame', 'freq'))
The draws below stay inside these ranges and needn't reach their ends.
All inputs are finite; a program needn't handle non-finite values.
Results may differ from the reference program's by a relative error of at most 0.0001.
Values sent between devices are 32-bit elements; how exact they have to be, the bound alone decides.
No kernel may reach another device: no remote copies, remote signals or barrier semaphores. Data moves between devices by JAX's collectives and lax.ppermute only.
A program may use at most 64 MiB of HBM per device.

```python
import math
import jax
import jax.numpy as jnp
from jax import lax

F = 8192
K = 128
ITERS = 2
FRAMES = 4096


def steps_of(rng, dims, pieces, low, high):
    def one(axis_at, blocks):
        heights = jax.random.uniform(jax.random.fold_in(jax.random.fold_in(rng, 6), axis_at), (blocks,), jnp.float32, low / len(pieces), high / len(pieces))
        return jnp.repeat(jnp.exp(heights), dims[axis_at] // blocks).reshape((-1,) + (1,) * (len(dims) - axis_at - 1))

    factor_of = one(*pieces[0])
    for cut in pieces[1:]:
        factor_of = factor_of * one(*cut)
    return factor_of


def setup_inputs(seed: int = 0) -> dict:
    streams_of = jax.random.split(jax.random.key(seed), 4)
    spectrum = jnp.clip(jnp.exp(math.log(10.0) - 4.6051702 * jax.random.uniform(streams_of[0], (F, FRAMES), jnp.float32) ** steps_of(streams_of[0], (F, FRAMES), ((0, 4), (1, 8)), -0.2, 0.2)), 0.1, 10.0)
    basis = jnp.clip(jnp.exp(math.log(0.5) - 3.218876 * jax.random.uniform(streams_of[1], (F, K), jnp.float32) ** steps_of(streams_of[1], (F, K), ((0, 32),), -0.2, 0.2)), 0.02, 0.5)
    activations = jnp.clip(jnp.exp(math.log(0.5) - 3.218876 * jax.random.uniform(streams_of[2], (FRAMES, K), jnp.float32) ** steps_of(streams_of[2], (FRAMES, K), ((0, 32),), -0.2, 0.2)), 0.02, 0.5)
    return dict(spectrum=spectrum, basis=basis, activations=activations)


def product(left, right, contract_left, contract_right):
    return lax.dot_general(left, right, (((contract_left,), (contract_right,)), ((), ())), precision=lax.Precision.HIGHEST, preferred_element_type=jnp.float32)


def reference(spectrum, basis, activations):
    basis_now = basis
    acts_now = activations
    for sweep in range(ITERS):
        quotient = spectrum / product(basis_now, acts_now, 1, 1)
        basis_total = jnp.sum(basis_now, axis=0)
        acts_now = acts_now * product(quotient, basis_now, 0, 0) / basis_total[None, :]
        quotient = spectrum / product(basis_now, acts_now, 1, 1)
        acts_total = jnp.sum(acts_now, axis=0)
        basis_now = basis_now * product(quotient, acts_now, 1, 0) / acts_total[None, :]
    return basis_now, acts_now
```

```python
import jax
import jax.numpy as jnp
from jax import lax
from jax.sharding import PartitionSpec as P

ITERS = 2


def product(left, right, contract_left, contract_right):
    return lax.dot_general(
        left,
        right,
        (((contract_left,), (contract_right,)), ((), ())),
        precision=lax.Precision.HIGH,
        preferred_element_type=jnp.float32,
    )


def ring_order(devices):
    count = len(devices)
    places = [getattr(device, "coords", None) for device in devices]
    natural = list(range(count))
    if any(place is None for place in places):
        return natural
    varying = [d for d in range(3) if len({place[d] for place in places}) > 1]
    if len(varying) != 2:
        return natural
    sizes = [sorted({place[d] for place in places}) for d in varying]
    if len(sizes[0]) * len(sizes[1]) != count:
        return natural
    index_of = {
        tuple(sizes[i].index(place[d]) for i, d in enumerate(varying)): at
        for at, place in enumerate(places)
    }
    rows, columns = len(sizes[0]), len(sizes[1])
    swap = rows % 2 == 1
    if swap:
        rows, columns = columns, rows
    if rows % 2 == 1:
        return natural
    cycle = [(r, 0) for r in range(rows)]
    for step, r in enumerate(reversed(range(rows))):
        across = range(1, columns) if step % 2 == 0 else range(columns - 1, 0, -1)
        cycle += [(r, c) for c in across]
    return [index_of[(c, r) if swap else (r, c)] for r, c in cycle]


def solution(mesh):
    frame_count, freq_count = mesh.shape["frame"], mesh.shape["freq"]
    names = list(mesh.axis_names)
    devices = mesh.devices
    if names.index("frame") != 0:
        devices = devices.T
    ring = ring_order([devices[i, 0] for i in range(frame_count)])
    place = [ring.index(i) for i in range(frame_count)]
    ahead, behind = frame_count // 2, (frame_count - 1) // 2

    def shift(value, by):
        pairs = [(ring[i], ring[(i + by) % frame_count]) for i in range(frame_count)]
        return lax.ppermute(value, "frame", pairs)

    def exchange(value, bit):
        return lax.ppermute(value, "freq", [(i, i ^ bit) for i in range(freq_count)])

    def per_device(spectrum, basis, activations):
        own_rows = basis.shape[0]
        frame_at = lax.axis_index("frame")
        freq_at = lax.axis_index("freq")
        core = freq_at % 2

        def rows_of(distance):
            owner = jnp.int32(0)
            for i in range(frame_count):
                there = ring[(place[i] + distance + frame_count) % frame_count]
                owner = jnp.where(frame_at == i, there, owner)
            return lax.dynamic_slice_in_dim(spectrum, owner * own_rows, own_rows, 0)

        distances = sorted(range(-ahead, behind + 1), key=lambda d: (abs(d), d))
        pieces = lax.optimization_barrier([rows_of(d) for d in distances])
        pieces = dict(zip(distances, pieces))

        def paired(own, other, bit):
            high = (freq_at & bit) != 0
            return jnp.concatenate(
                [jnp.where(high, other, own), jnp.where(high, own, other)], 0
            )

        def gather_acts(own):
            bit = 1
            while bit < freq_count:
                own = paired(own, exchange(own, bit), bit)
                bit *= 2
            return own

        def gather_basis(own):
            blocks = {0: own}
            for hop in range(1, ahead + 1):
                blocks[-hop] = shift(blocks[-hop + 1], 1)
                if hop <= behind:
                    blocks[hop] = shift(blocks[hop - 1], -1)
            return blocks

        def quotient(block, acts, distance):
            return pieces[distance] / product(block, acts, 1, 1)

        acts = gather_acts(activations)
        for sweep in range(ITERS):
            blocks = gather_basis(basis)
            numerator, total = 0.0, 0.0
            for distance in distances:
                block = blocks[distance]
                numerator += product(quotient(block, acts, distance), block, 0, 0)
                total += jnp.sum(block, axis=0, keepdims=True)
            half = numerator.shape[0] // 2
            total = jnp.broadcast_to(total, (8, total.shape[1]))
            low, high = numerator[:half], numerator[half:]
            mine = jnp.concatenate([jnp.where(core == 0, low, high), total], 0)
            other = jnp.concatenate([jnp.where(core == 0, high, low), total], 0)
            mine = mine + exchange(other, 1)
            bit = 2
            while bit < freq_count:
                mine = mine + exchange(mine, bit)
                bit *= 2
            old = jnp.where(core == 0, acts[:half], acts[half:])
            new = old * mine[:half] / mine[half : half + 1]
            acts = paired(new, exchange(new, 1), 1)

            acts_total = jnp.broadcast_to(
                jnp.sum(acts, axis=0, keepdims=True), (8, acts.shape[1])
            )

            def share(distance):
                q = quotient(blocks[distance], acts, distance)
                return jnp.concatenate([product(q, acts, 1, 0), acts_total], 0)

            forward, backward = None, None
            for hop in range(ahead, 0, -1):
                term = share(hop if hop <= behind else -hop)
                forward = term if forward is None else forward + term
                if hop <= behind:
                    term = share(-hop)
                    backward = term if backward is None else backward + term
                    forward, backward = lax.optimization_barrier((forward, backward))
                    backward = shift(backward, -1)
                forward = shift(forward, 1)
            summed = share(0) + forward
            if backward is not None:
                summed = summed + backward
            basis = basis * summed[:own_rows] / summed[own_rows : own_rows + 1]
        own_frames = activations.shape[0]
        acts_owned = lax.dynamic_slice_in_dim(acts, freq_at * own_frames, own_frames, 0)
        return basis, acts_owned

    return jax.shard_map(
        per_device,
        mesh=mesh,
        in_specs=(P("freq", "frame"), P(("freq", "frame"), None), P(("frame", "freq"), None)),
        out_specs=(P(("freq", "frame"), None), P(("frame", "freq"), None)),
        check_vma=False,
    )
```

```python
import functools

import jax
import jax.numpy as jnp
from jax import lax
from jax.experimental import pallas as pl
from jax.experimental.pallas import tpu as pltpu
from jax.sharding import PartitionSpec as P

ITERS = 2
PAD = 8
F32, BF16 = jnp.float32, jnp.bfloat16
VMEM = pl.BlockSpec(memory_space=pltpu.VMEM)
PARAMS = pltpu.CompilerParams(vmem_limit_bytes=12 * 2**20)


def ring_order(devices):
    count = len(devices)
    places = [getattr(device, "coords", None) for device in devices]
    natural = list(range(count))
    if any(place is None for place in places):
        return natural
    varying = [d for d in range(3) if len({place[d] for place in places}) > 1]
    if len(varying) != 2:
        return natural
    sizes = [sorted({place[d] for place in places}) for d in varying]
    if len(sizes[0]) * len(sizes[1]) != count:
        return natural
    index_of = {
        tuple(sizes[i].index(place[d]) for i, d in enumerate(varying)): at
        for at, place in enumerate(places)
    }
    rows, columns = len(sizes[0]), len(sizes[1])
    swap = rows % 2 == 1
    if swap:
        rows, columns = columns, rows
    if rows % 2 == 1:
        return natural
    cycle = [(r, 0) for r in range(rows)]
    for step, r in enumerate(reversed(range(rows))):
        across = range(1, columns) if step % 2 == 0 else range(columns - 1, 0, -1)
        cycle += [(r, c) for c in across]
    return [index_of[(c, r) if swap else (r, c)] for r, c in cycle]


def pair(value):
    high = value.astype(BF16)
    return high, (value - high.astype(F32)).astype(BF16)


def dot(left, right, contract_left, contract_right):
    return lax.dot_general(
        left,
        right,
        (((contract_left,), (contract_right,)), ((), ())),
        preferred_element_type=F32,
    )


def acts_pair(acts):
    high, low = pair(acts)
    return high, low, jnp.concatenate([high, high], 1)


def quotient(rows, basis_high, basis_both, acts_low, acts_twice):
    estimate = dot(basis_both, acts_twice, 1, 1) + dot(basis_high, acts_low, 1, 1)
    guess = pltpu.reciprocal(estimate, approx=True)
    return rows * (guess * (2.0 - estimate * guess))


def basis_pair(block):
    high, low = pair(block)
    return high, jnp.concatenate([high, low], 1)


def rows_at(spectrum, owners, count):
    at = lax.axis_index("frame")
    owner = jnp.int32(0)
    for frame, value in enumerate(owners):
        owner = jnp.where(at == frame, value, owner)
    return spectrum[pl.ds(pl.multiple_of(owner * count, count), count), :]


def acts_numerator(owners, blocks, spectrum, acts, start):
    rank = acts.shape[1]
    _, acts_low, acts_twice = acts_pair(acts[...])
    numerator = None if start is None else start[: acts.shape[0]]
    total = None if start is None else start[acts.shape[0] :]
    for owner, block in zip(owners, blocks):
        value = block[...]
        high, both = basis_pair(value)
        row = rows_at(spectrum, owner, value.shape[0])
        q_high, q_low = pair(quotient(row, high, both, acts_low, acts_twice))
        wide = dot(q_high, both, 0, 0)
        part = wide[:, :rank] + wide[:, rank:] + dot(q_low, high, 0, 0)
        sums = jnp.broadcast_to(jnp.sum(value, 0, keepdims=True), (PAD, rank))
        numerator = part if numerator is None else numerator + part
        total = sums if total is None else total + sums
    return numerator, total


def gather_kernel(owners, spectrum, acts, *refs):
    count = len(owners)
    blocks, start, out = refs[:count], refs[count:-1], refs[-1]
    numerator, total = acts_numerator(owners, blocks, spectrum, acts, start[0] if start else None)
    out[: acts.shape[0]] = numerator
    out[acts.shape[0] :] = total


def last_gather_kernel(owners, spectrum, acts, *refs):
    count = len(owners)
    blocks, start, (mine, other) = refs[:count], refs[count:-2], refs[-2:]
    numerator, total = acts_numerator(owners, blocks, spectrum, acts, start[0] if start else None)
    half = acts.shape[0] // 2
    second = lax.axis_index("freq") % 2 == 1
    low, high = numerator[:half], numerator[half:]
    mine[:half] = jnp.where(second, high, low)
    other[:half] = jnp.where(second, low, high)
    mine[half:] = total
    other[half:] = total


def scatter_kernel(owners, spectrum, acts, *refs):
    count = len(owners)
    blocks, outs = refs[:count], refs[count:]
    value = acts[...]
    rank = value.shape[1]
    acts_high, acts_low, acts_twice = acts_pair(value)
    acts_both = jnp.concatenate([acts_high, acts_low], 1)
    total = jnp.broadcast_to(jnp.sum(value, 0, keepdims=True), (PAD, rank))
    for owner, block, out in zip(owners, blocks, outs):
        high, both = basis_pair(block[...])
        row = rows_at(spectrum, owner, block.shape[0])
        q_high, q_low = pair(quotient(row, high, both, acts_low, acts_twice))
        wide = dot(q_high, acts_both, 1, 0)
        out[: block.shape[0]] = wide[:, :rank] + wide[:, rank:] + dot(q_low, acts_high, 1, 0)
        out[block.shape[0] :] = total


def ordered_kernel(axis_bit, own, other, out):
    count = own.shape[0]
    high = (lax.axis_index("freq") // axis_bit) % 2
    out[pl.ds(pl.multiple_of(high * count, count), count), :] = own[...]
    out[pl.ds(pl.multiple_of((1 - high) * count, count), count), :] = other[...]


def update_kernel(acts, mine, came, out):
    half = out.shape[0]
    second = lax.axis_index("freq") % 2
    old = acts[pl.ds(pl.multiple_of(second * half, half), half), :]
    total = mine[half : half + 1] + came[half : half + 1]
    out[...] = old * (mine[:half] + came[:half]) / total


def own_kernel(acts, out):
    count = out.shape[0]
    start = pl.multiple_of(lax.axis_index("freq") * count, count)
    out[...] = acts[pl.ds(start, count), :]


def in_vmem(*shape):
    return pltpu.VMEM(shape, F32)


def solution(mesh):
    frame_count, freq_count = mesh.shape["frame"], mesh.shape["freq"]
    devices = mesh.devices
    if mesh.axis_names[0] != "frame":
        devices = devices.T
    ring = ring_order([devices[i, 0] for i in range(frame_count)])
    place = [ring.index(i) for i in range(frame_count)]
    reach = (frame_count - 1) // 2
    opposite = frame_count // 2 if frame_count % 2 == 0 else 0

    def moved(by):
        return [(ring[i], ring[(i + by) % frame_count]) for i in range(frame_count)]

    def shift(value, by):
        return lax.ppermute(value, "frame", moved(by))

    def exchange(value, bit):
        return lax.ppermute(value, "freq", [(i, i ^ bit) for i in range(freq_count)])

    def tied(value, *others):
        return lax.optimization_barrier((value, *others))[0]

    def per_device(spectrum, basis, activations):
        own_rows, rank = basis.shape
        own_frames = activations.shape[0]
        frames = own_frames * freq_count
        half = frames // 2
        distances = list(range(-reach, reach + 1)) + ([opposite] if opposite else [])
        owner_at = [
            [ring[(place[i] + d) % frame_count] for i in range(frame_count)] for d in distances
        ]
        owner_at = dict(zip(distances, owner_at))
        spectrum = pltpu.with_memory_space_constraint(spectrum, pltpu.VMEM)

        def cost(count):
            work = count * own_rows * frames
            return pl.CostEstimate(flops=16 * work * rank, bytes_accessed=4 * work, transcendentals=work)

        def gathered(blocks, which, acts, start, last):
            operands = [spectrum, acts] + [blocks[d] for d in which]
            if start is not None:
                operands.append(start)
            shapes = [in_vmem(half + PAD, rank)] * 2 if last else [in_vmem(frames + PAD, rank)]
            kernel = last_gather_kernel if last else gather_kernel
            return pl.pallas_call(
                functools.partial(kernel, [owner_at[d] for d in which]),
                out_shape=shapes,
                in_specs=[VMEM] * len(operands),
                out_specs=[VMEM] * len(shapes),
                compiler_params=PARAMS,
                cost_estimate=cost(len(which)),
                name="gather_last" if last else "gather_part",
            )(*operands)

        def scattered(blocks, which, acts):
            operands = [spectrum, acts] + [blocks[d] for d in which]
            return pl.pallas_call(
                functools.partial(scatter_kernel, [owner_at[d] for d in which]),
                out_shape=[in_vmem(own_rows + PAD, rank) for _ in which],
                in_specs=[VMEM] * len(operands),
                out_specs=[VMEM] * len(which),
                compiler_params=PARAMS,
                cost_estimate=cost(len(which)),
                name="scatter_part",
            )(*operands)

        def small(kernel, name, shape, *operands):
            return pl.pallas_call(
                kernel,
                out_shape=shape,
                in_specs=[VMEM] * len(operands),
                out_specs=VMEM,
                compiler_params=PARAMS,
                name=name,
            )(*operands)

        def ordered(own, other, bit):
            shape = in_vmem(2 * own.shape[0], rank)
            return small(functools.partial(ordered_kernel, bit), "ordered", shape, own, other)

        acts = activations
        bit = 1
        while bit < freq_count:
            acts = ordered(acts, exchange(acts, bit), bit)
            bit *= 2

        for sweep in range(ITERS):
            blocks = {0: basis}
            for hop in range(1, reach + 1):
                blocks[-hop] = shift(blocks[1 - hop], 1)
                blocks[hop] = shift(blocks[hop - 1], -1)
            numerator = None
            if reach:
                (numerator,) = gathered(blocks, [0], acts, None, False)
            if opposite:
                blocks[opposite] = shift(basis, opposite)
            for hop in range(1, reach):
                (numerator,) = gathered(blocks, [-hop, hop], acts, numerator, False)
            last = ([opposite] if opposite else []) + ([-reach, reach] if reach else [0])
            mine, other = gathered(blocks, last, acts, numerator, True)
            mine = mine + exchange(other, 1)
            bit = 2
            while 2 * bit < freq_count:
                mine = mine + exchange(mine, bit)
                bit *= 2
            new = small(update_kernel, "update", in_vmem(half, rank), acts, mine, exchange(mine, bit))
            acts = ordered(new, exchange(new, 1), 1)

            arrived = []
            if reach:
                forward, backward = scattered(blocks, [reach, -reach], acts)
                far_terms = scattered(blocks, [opposite], acts) if opposite else []
                for hop in range(reach, 0, -1):
                    came_forward, came_backward = shift(forward, 1), shift(backward, -1)
                    if hop == 1:
                        arrived = [came_forward, came_backward]
                        break
                    to_forward, to_backward = scattered(blocks, [hop - 1, 1 - hop], acts)
                    forward = tied(came_forward, backward) + to_forward
                    backward = tied(came_backward, forward) + to_backward
                arrived += [shift(term, opposite) for term in far_terms]
            elif opposite:
                arrived = [shift(scattered(blocks, [opposite], acts)[0], opposite)]
            (summed,) = scattered(blocks, [0], acts)
            for value in arrived:
                summed = summed + value
            basis = basis * summed[:own_rows] / summed[own_rows : own_rows + 1]
        shape = jax.ShapeDtypeStruct((own_frames, rank), F32)
        acts_owned = small(own_kernel, "own", shape, acts)
        return basis, acts_owned

    return jax.shard_map(
        per_device,
        mesh=mesh,
        in_specs=(P("freq", "frame"), P(("freq", "frame"), None), P(("frame", "freq"), None)),
        out_specs=(P(("freq", "frame"), None), P(("frame", "freq"), None)),
        check_vma=False,
    )
```
